32 devices in a mesh: groups: 2 (over x), row: 8 (over z, y), col: 2 (over core).
Axes of the slice: x: 2, y: 2, z: 4, core: 2. Of those that a mesh axis runs over, the one named last changes fastest.
Arguments:
- queries: bfloat16 [4096, 2560], P(('groups', 'row', 'col')), parts along dimension 0, may hold values from -32 to 32
- keys: bfloat16 [4096, 2560], P(('groups', 'row', 'col')), parts along dimension 0, may hold values from -6 to 6
- values: bfloat16 [4096, 2560], P(('groups', 'row', 'col')), parts along dimension 0, may hold values from -6 to 6
- pattern: int32 [16, 5], P('groups'), parts along dimension 0, may hold values from 0 to 1, as said below
Outputs:
- attended: bfloat16 [4096, 2560], P(('groups', 'row', 'col')), parts along dimension 0
The draws below stay inside these ranges and needn't reach their ends.
There are 2 independent parts, one for each index of `groups`. The reference program is written for one: setup_inputs(seed, part) draws one part's arguments, and reference() takes and returns one part's arrays. A program takes and returns all parts, laid end to end along the dimension named above; each array names one. Nothing has to cross between parts.
Inputs may be any that keep to these rules, and one draw needn't show every extreme that they name: pattern[r, 0] is 1; pattern[r, j] is 0 where r + off_j lies outside 0 .. 7, or where off_j is -1 or +1 and r + off_j lies in another band of 4 tile rows.
All inputs are finite; a program needn't handle non-finite values.
Results may differ from the reference program's by a relative error of at most 0.0045.
Values may be sent and summed in bfloat16 or wider, within the bound.
A program may use at most 64 MiB of HBM per device.

```python
import math
import jax
import jax.numpy as jnp
from jax import lax

HEADS = 20
HD = 128
TILE_H = 4
WIDTH = 2560
TILE_ROWS = 8
TOKENS = 2048


def shared_draw(key):
    base = jax.random.fold_in(key, 17)
    first = jax.random.fold_in(base, 0)
    third = jax.random.fold_in(base, 2)
    width = HEADS * HD
    shape = (TOKENS, width)
    keys_all = jnp.clip(jax.random.normal(first, shape, jnp.float32), -6.0, 6.0)
    queries_all = jnp.clip(jax.random.normal(third, shape, jnp.float32), -6.0, 6.0)
    return (queries_all, keys_all)


def draw_queries(key, part):
    return shared_draw(key)[0].astype(jnp.bfloat16)


def draw_keys(key, part):
    return shared_draw(key)[1].astype(jnp.bfloat16)


def draw_pattern(key, part):
    first, second = jax.random.split(jax.random.fold_in(key, 29))
    row_numbers = jnp.arange(TILE_ROWS, dtype=jnp.int32)[:, None]
    offsets = jnp.array([0, -1, 1, -TILE_H, TILE_H], jnp.int32)[None, :]
    target = row_numbers + offsets
    inside = (target >= 0) & (target < TILE_ROWS)
    same_band = (jnp.abs(offsets) != 1) | (target // TILE_H == row_numbers // TILE_H)
    appetite = jax.random.randint(first, (TILE_ROWS, 1), 0, 5)
    rolls = jax.random.randint(second, (TILE_ROWS, 5), 0, 4)
    chosen = (rolls < appetite) & inside & same_band | (offsets == 0)
    return chosen.astype(jnp.int32)


def steps_of(own_key, dims, shards, smallest, high):
    def one(dim, parts):
        draws = jax.random.uniform(jax.random.fold_in(jax.random.fold_in(own_key, 6), dim), (parts,), jnp.float32, smallest / len(shards), high / len(shards))
        return jnp.repeat(jnp.exp(draws), dims[dim] // parts).reshape((-1,) + (1,) * (len(dims) - dim - 1))

    factor_of = one(*shards[0])
    for cut in shards[1:]:
        factor_of = factor_of * one(*cut)
    return factor_of


def scatter_about(own_key, shape, scale, bound, cuts=(), held_as=jnp.bfloat16):
    values = scale * jax.random.normal(own_key, shape, jnp.float32)
    if cuts:
        values = values * steps_of(own_key, shape, cuts, -0.22, 0.18)
    return jnp.clip(values, -bound, bound).astype(held_as)


def setup_inputs(seed: int = 0, part: int = 0) -> dict:
    key_list = jax.random.split(jax.random.key(seed), 5)
    part_splits = jax.random.split(jax.random.fold_in(key_list[4], part), 5)
    return {
        "queries": draw_queries(jax.random.fold_in(jax.random.fold_in(key_list[4], part), 71), part),
        "keys": draw_keys(jax.random.fold_in(jax.random.fold_in(key_list[4], part), 71), part),
        "values": scatter_about(part_splits[2], (TOKENS, WIDTH), 1.0, 6.0, ((0, 16),)),
        "pattern": draw_pattern(jax.random.fold_in(jax.random.fold_in(key_list[4], part), 71), part),
    }


far_below = -1e+30

def block_terms(query_block, key_block, value_block):
    query_float = query_block.astype(jnp.float32)
    key_float = key_block.astype(jnp.float32)
    value_float = value_block.astype(jnp.float32)
    scores = jnp.einsum('qhd,khd->hqk', query_float, key_float, precision=lax.Precision.HIGHEST) * (1.0 / math.sqrt(HD))
    block_max = lax.optimization_barrier(jnp.max(scores, axis=2))
    weights = jnp.exp(scores - block_max[:, :, None])
    block_total = lax.optimization_barrier(jnp.sum(weights, axis=2))
    rounded = lax.optimization_barrier(weights.astype(jnp.bfloat16)).astype(jnp.float32)
    block_out = jnp.einsum('hqk,khd->qhd', rounded, value_float, precision=lax.Precision.HIGHEST)
    return (block_out, block_max.T, block_total.T)

def reference(queries, keys, values, pattern):
    row_tokens = TOKENS // TILE_ROWS
    query_rows = queries.reshape(TILE_ROWS, row_tokens, HEADS, HD)
    key_rows = keys.reshape(TILE_ROWS, row_tokens, HEADS, HD)
    value_rows = values.reshape(TILE_ROWS, row_tokens, HEADS, HD)
    offsets = [0, -1, 1, -TILE_H, TILE_H]

    def one_row(row_number):
        query_block = lax.dynamic_index_in_dim(query_rows, row_number, 0, keepdims=False)
        outs_list = []
        maxes_list = []
        totals_list = []
        for number in range(5):
            key_index = jnp.clip(row_number + offsets[number], 0, TILE_ROWS - 1).astype(jnp.int32)
            key_block = lax.dynamic_index_in_dim(key_rows, key_index, 0, keepdims=False)
            value_block = lax.dynamic_index_in_dim(value_rows, key_index, 0, keepdims=False)
            block_out, block_max, block_total = block_terms(query_block, key_block, value_block)
            is_live = pattern[row_number, number] == 1
            outs_list.append(jnp.where(is_live, block_out, jnp.float32(0.0)))
            maxes_list.append(jnp.where(is_live, block_max, jnp.float32(far_below)))
            totals_list.append(jnp.where(is_live, block_total, jnp.float32(0.0)))
        outs_all = jnp.stack(outs_list)
        maxes_all = jnp.stack(maxes_list)
        totals_all = jnp.stack(totals_list)
        top_max = lax.optimization_barrier(jnp.max(maxes_all, axis=0))
        factors = jnp.exp(maxes_all - top_max)
        numerator = lax.optimization_barrier(jnp.sum(factors[..., None] * outs_all, axis=0))
        denominator = lax.optimization_barrier(jnp.sum(factors * totals_all, axis=0))
        result = (numerator / denominator[..., None]).astype(jnp.bfloat16)
        return result.reshape(row_tokens, HEADS * HD)
    attended = lax.map(one_row, jnp.arange(TILE_ROWS, dtype=jnp.int32))
    return attended.reshape(TOKENS, HEADS * HD)
```

```python
import functools
import math

import jax
import jax.numpy as jnp
from jax import lax
from jax.experimental import pallas as pl
from jax.experimental.pallas import tpu as pltpu
from jax.sharding import PartitionSpec as P

HEADS = 20
HD = 128
TILE_H = 4
OFFSETS = (0, -1, 1, -TILE_H, TILE_H)
GROUP = 1

MESH = pl.DeviceIdType.MESH
FAR = 1e30
TO_EXP2 = math.log2(math.e) / math.sqrt(HD)


def kernel(
    rows, cols, q_hbm, k_hbm, v_hbm, pattern_ref, out_ref,
    q_all, kv, staged, acc, top, total,
    near_send, near_recv, local_sem, far_send, far_recv, out_send, out_recv,
):
    row = lax.axis_index("row")
    col = lax.axis_index("col")
    tokens = q_hbm.shape[0]
    half = q_hbm.shape[1] // cols
    step = GROUP * HD
    chunks = half // step
    own_tokens = pl.ds(pl.multiple_of(col * tokens, tokens), tokens)

    def has(offset):
        if offset == -1:
            return lax.rem(row, TILE_H) != 0
        if offset == 1:
            return (lax.rem(row, TILE_H) != TILE_H - 1) & (row + 1 < rows)
        if offset < 0:
            return row >= -offset
        return row + offset < rows

    def other_col(d):
        return lax.rem(col + d, cols)

    def wide(which, i):
        return pl.ds(pl.multiple_of(which * half + i * step, HD), step)

    def narrow(i):
        return pl.ds(pl.multiple_of(i * step, HD), step)

    barrier = pltpu.get_barrier_semaphore()
    for d in range(1, cols):
        pl.semaphore_signal(barrier, inc=1, device_id={"col": other_col(d)}, device_id_type=MESH)
    for j in range(1, 5):
        @pl.when(has(-OFFSETS[j]))
        def _():
            pl.semaphore_signal(
                barrier, inc=1, device_id={"row": row - OFFSETS[j]}, device_id_type=MESH
            )
    peers = cols - 1
    for j in range(1, 5):
        peers = peers + has(-OFFSETS[j]).astype(jnp.int32)
    pl.semaphore_wait(barrier, peers)

    def near_parts(i):
        return (
            (0, k_hbm, kv.at[0, 0, own_tokens, narrow(i)]),
            (1, v_hbm, kv.at[0, 1, own_tokens, narrow(i)]),
            (2, q_hbm, q_all.at[own_tokens, narrow(i)]),
        )

    def near_copies(i, which):
        for n, src, dst in near_parts(i):
            if n in which:
                for d in range(1, cols):
                    yield pltpu.make_async_remote_copy(
                        src_ref=src.at[:, wide(other_col(d), i)],
                        dst_ref=dst,
                        send_sem=near_send.at[n, d - 1, i],
                        recv_sem=near_recv.at[n, d - 1, i],
                        device_id={"col": other_col(d)},
                        device_id_type=MESH,
                    )

    def local_copies(i, which):
        for n, src, dst in near_parts(i):
            if n in which:
                yield pltpu.make_async_copy(
                    src.at[:, wide(col, i)], dst, local_sem.at[n, i]
                )

    def far_copy(j, i):
        return pltpu.make_async_remote_copy(
            src_ref=kv.at[0, :, :, narrow(i)],
            dst_ref=kv.at[j, :, :, narrow(i)],
            send_sem=far_send.at[j - 1, i],
            recv_sem=far_recv.at[j - 1, i],
            device_id={"row": row - OFFSETS[j]},
            device_id_type=MESH,
        )

    for which in ((0, 1), (2,)):
        @pl.loop(0, chunks)
        def _(i):
            for copy in near_copies(i, which):
                copy.start()
            for copy in local_copies(i, which):
                copy.start()

    @pl.loop(0, chunks)
    def _(i):
        for copy in near_copies(i, (0, 1)):
            copy.wait_recv()
        for copy in local_copies(i, (0, 1)):
            copy.wait()
        for j in (3, 4, 1, 2):
            @pl.when(has(-OFFSETS[j]))
            def _():
                far_copy(j, i).start()

    def out_copies(i):
        for d in range(1, cols):
            to = other_col(d)
            yield pltpu.make_async_remote_copy(
                src_ref=staged.at[pl.ds(pl.multiple_of(to * tokens, tokens), tokens), narrow(i)],
                dst_ref=out_ref.at[:, wide(col, i)],
                send_sem=out_send.at[d - 1, i],
                recv_sem=out_recv.at[d - 1, i],
                device_id={"col": to},
                device_id_type=MESH,
            )

    @pl.loop(0, chunks)
    def _(i):
        for copy in near_copies(i, (2,)):
            copy.wait_recv()
        for copy in local_copies(i, (2,)):
            copy.wait()

        def block(j, g):
            head = pl.ds(pl.multiple_of(i * step + g * HD, HD), HD)
            scores = lax.dot_general(
                q_all[:, head], kv[j, 0, :, head], (((1,), (1,)), ((), ())),
                preferred_element_type=jnp.float32,
            )
            peak = jnp.max(scores, axis=1, keepdims=True)
            if j == 0:
                weights = jnp.exp2((scores - peak) * TO_EXP2)
                here = jnp.sum(weights, axis=1, keepdims=True)
                out = jnp.dot(
                    weights.astype(jnp.bfloat16), kv[j, 1, :, head],
                    preferred_element_type=jnp.float32,
                )
                top[g] = peak
                total[g] = here
                acc[g] = out
            else:
                live = pattern_ref[row, j] == 1
                before = top[g]
                after = jnp.where(live, jnp.maximum(before, peak), before)
                weights = jnp.exp2((scores - jnp.where(live, after, FAR)) * TO_EXP2)
                here = jnp.sum(weights, axis=1, keepdims=True)
                out = jnp.dot(
                    weights.astype(jnp.bfloat16), kv[j, 1, :, head],
                    preferred_element_type=jnp.float32,
                )
                factor = jnp.exp2((before - after) * TO_EXP2)
                top[g] = after
                total[g] = total[g] * factor + here
                acc[g] = acc[g] * factor + out

        for g in range(GROUP):
            block(0, g)
        for j in (1, 2, 3, 4):
            @pl.when(has(OFFSETS[j]))
            def _():
                far_copy(j, i).wait_recv()
                for g in range(GROUP):
                    block(j, g)
        for g in range(GROUP):
            head = pl.ds(pl.multiple_of(i * step + g * HD, HD), HD)
            staged[:, head] = (acc[g] / total[g]).astype(jnp.bfloat16)
        out_ref[:, wide(col, i)] = staged[own_tokens, narrow(i)]
        for copy in out_copies(i):
            copy.start()

    @pl.loop(0, chunks)
    def _(i):
        for copy in near_copies(i, (0, 1, 2)):
            copy.wait_send()
        for j in range(1, 5):
            @pl.when(has(-OFFSETS[j]))
            def _():
                far_copy(j, i).wait_send()
        for copy in out_copies(i):
            copy.wait()


def shards(rows, cols, queries, keys, values, pattern):
    tokens, width = queries.shape
    half = width // cols
    chunks = half // (GROUP * HD)
    whole = tokens * cols
    dma = pltpu.SemaphoreType.DMA
    return pl.pallas_call(
        functools.partial(kernel, rows, cols),
        out_shape=jax.ShapeDtypeStruct((tokens, width), jnp.bfloat16),
        in_specs=[pl.BlockSpec(memory_space=pl.ANY)] * 3
        + [pl.BlockSpec(memory_space=pltpu.SMEM)],
        out_specs=pl.BlockSpec(memory_space=pltpu.VMEM),
        scratch_shapes=[
            pltpu.VMEM((whole, half), jnp.bfloat16),
            pltpu.VMEM((5, 2, whole, half), jnp.bfloat16),
            pltpu.VMEM((whole, half), jnp.bfloat16),
            pltpu.VMEM((GROUP, whole, HD), jnp.float32),
            pltpu.VMEM((GROUP, whole, 1), jnp.float32),
            pltpu.VMEM((GROUP, whole, 1), jnp.float32),
            dma((3, cols - 1, chunks)),
            dma((3, cols - 1, chunks)),
            dma((3, chunks)),
            dma((4, chunks)),
            dma((4, chunks)),
            dma((cols - 1, chunks)),
            dma((cols - 1, chunks)),
        ],
        compiler_params=pltpu.CompilerParams(
            collective_id=0, has_side_effects=True, vmem_limit_bytes=32 * 1024 * 1024
        ),
        cost_estimate=pl.CostEstimate(
            flops=4 * 4 * whole * whole * half,
            bytes_accessed=8 * tokens * width,
            transcendentals=4 * whole * whole * half // HD,
        ),
    )(queries, keys, values, pattern)


def solution(mesh):
    split = P(("groups", "row", "col"), None)
    return jax.shard_map(
        functools.partial(shards, mesh.shape["row"], mesh.shape["col"]),
        mesh=mesh,
        in_specs=(split, split, split, P("groups", None)),
        out_specs=split,
        check_vma=False,
    )
```

```python
import functools
import math

import jax
import jax.numpy as jnp
from jax import lax
from jax.experimental import pallas as pl
from jax.experimental.pallas import tpu as pltpu
from jax.sharding import PartitionSpec as P

HEADS = 20
HD = 128
TILE_H = 4
OFFSETS = (0, -1, 1, -TILE_H, TILE_H)
GROUP = 2

MESH = pl.DeviceIdType.MESH
FAR = 1e30
TO_EXP2 = math.log2(math.e) / math.sqrt(HD)


def kernel(
    rows, cols, q_hbm, k_hbm, v_hbm, pattern_ref, out_ref,
    q_all, kv, staged, acc, top, total,
    near_send, near_recv, local_sem, far_send, far_recv, out_send, out_recv,
):
    row = lax.axis_index("row")
    col = lax.axis_index("col")
    tokens = q_hbm.shape[0]
    half = q_hbm.shape[1] // cols
    step = GROUP * HD
    chunks = half // step
    own_tokens = pl.ds(pl.multiple_of(col * tokens, tokens), tokens)

    def has(offset):
        if offset == -1:
            return lax.rem(row, TILE_H) != 0
        if offset == 1:
            return (lax.rem(row, TILE_H) != TILE_H - 1) & (row + 1 < rows)
        if offset < 0:
            return row >= -offset
        return row + offset < rows

    def other_col(d):
        return lax.rem(col + d, cols)

    def wide(which, i):
        return pl.ds(pl.multiple_of(which * half + i * step, HD), step)

    def narrow(i):
        return pl.ds(pl.multiple_of(i * step, HD), step)

    barrier = pltpu.get_barrier_semaphore()
    for d in range(1, cols):
        pl.semaphore_signal(barrier, inc=1, device_id={"col": other_col(d)}, device_id_type=MESH)
    for j in range(1, 5):
        @pl.when(has(-OFFSETS[j]))
        def _():
            for d in range(cols):
                pl.semaphore_signal(
                    barrier, inc=1,
                    device_id={"row": row - OFFSETS[j], "col": other_col(d)},
                    device_id_type=MESH,
                )
    peers = cols - 1
    for j in range(1, 5):
        peers = peers + cols * has(-OFFSETS[j]).astype(jnp.int32)
    pl.semaphore_wait(barrier, peers)

    def near_parts(i):
        return (
            (0, k_hbm, kv.at[0, 0, own_tokens, narrow(i)]),
            (1, v_hbm, kv.at[0, 1, own_tokens, narrow(i)]),
            (2, q_hbm, q_all.at[own_tokens, narrow(i)]),
        )

    def near_copies(i, which):
        for n, src, dst in near_parts(i):
            if n in which:
                for d in range(1, cols):
                    yield pltpu.make_async_remote_copy(
                        src_ref=src.at[:, wide(other_col(d), i)],
                        dst_ref=dst,
                        send_sem=near_send.at[n, d - 1, i],
                        recv_sem=near_recv.at[n, d - 1, i],
                        device_id={"col": other_col(d)},
                        device_id_type=MESH,
                    )

    def local_copies(i, which):
        for n, src, dst in near_parts(i):
            if n in which:
                yield pltpu.make_async_copy(
                    src.at[:, wide(col, i)], dst, local_sem.at[n, i]
                )

    def far_copies(j, i):
        for d in range(cols):
            for n, src in ((0, k_hbm), (1, v_hbm)):
                yield pltpu.make_async_remote_copy(
                    src_ref=src.at[:, wide(other_col(d), i)],
                    dst_ref=kv.at[j, n, own_tokens, narrow(i)],
                    send_sem=far_send.at[j - 1, n, d, i],
                    recv_sem=far_recv.at[j - 1, n, d, i],
                    device_id={"row": row - OFFSETS[j], "col": other_col(d)},
                    device_id_type=MESH,
                )

    @pl.loop(0, chunks)
    def _(i):
        for j in (3, 4, 1, 2):
            @pl.when(has(-OFFSETS[j]))
            def _():
                for copy in far_copies(j, i):
                    copy.start()
        for copy in near_copies(i, (0, 1, 2)):
            copy.start()
        for copy in local_copies(i, (0, 1, 2)):
            copy.start()

    def out_copies(i):
        for d in range(1, cols):
            to = other_col(d)
            yield pltpu.make_async_remote_copy(
                src_ref=staged.at[pl.ds(pl.multiple_of(to * tokens, tokens), tokens), narrow(i)],
                dst_ref=out_ref.at[:, wide(col, i)],
                send_sem=out_send.at[d - 1, i],
                recv_sem=out_recv.at[d - 1, i],
                device_id={"col": to},
                device_id_type=MESH,
            )

    @pl.loop(0, chunks)
    def _(i):
        for copy in near_copies(i, (0, 1, 2)):
            copy.wait_recv()
        for copy in local_copies(i, (0, 1, 2)):
            copy.wait()

        def block(j, g):
            head = pl.ds(pl.multiple_of(i * step + g * HD, HD), HD)
            scores = lax.dot_general(
                q_all[:, head], kv[j, 0, :, head], (((1,), (1,)), ((), ())),
                preferred_element_type=jnp.float32,
            )
            peak = jnp.max(scores, axis=1, keepdims=True)
            if j == 0:
                weights = jnp.exp2((scores - peak) * TO_EXP2)
                here = jnp.sum(weights, axis=1, keepdims=True)
                out = jnp.dot(
                    weights.astype(jnp.bfloat16), kv[j, 1, :, head],
                    preferred_element_type=jnp.float32,
                )
                top[g] = peak
                total[g] = here
                acc[g] = out
            else:
                live = pattern_ref[row, j] == 1
                before = top[g]
                after = jnp.where(live, jnp.maximum(before, peak), before)
                weights = jnp.exp2((scores - jnp.where(live, after, FAR)) * TO_EXP2)
                here = jnp.sum(weights, axis=1, keepdims=True)
                out = jnp.dot(
                    weights.astype(jnp.bfloat16), kv[j, 1, :, head],
                    preferred_element_type=jnp.float32,
                )
                factor = jnp.exp2((before - after) * TO_EXP2)
                top[g] = after
                total[g] = total[g] * factor + here
                acc[g] = acc[g] * factor + out

        for g in range(GROUP):
            block(0, g)
        for j in (1, 2, 3, 4):
            @pl.when(has(OFFSETS[j]))
            def _():
                for copy in far_copies(j, i):
                    copy.wait_recv()
                for g in range(GROUP):
                    block(j, g)
        for g in range(GROUP):
            head = pl.ds(pl.multiple_of(i * step + g * HD, HD), HD)
            staged[:, head] = (acc[g] / total[g]).astype(jnp.bfloat16)
        out_ref[:, wide(col, i)] = staged[own_tokens, narrow(i)]
        for copy in out_copies(i):
            copy.start()

    @pl.loop(0, chunks)
    def _(i):
        for copy in near_copies(i, (0, 1, 2)):
            copy.wait_send()
        for j in range(1, 5):
            @pl.when(has(-OFFSETS[j]))
            def _():
                for copy in far_copies(j, i):
                    copy.wait_send()
        for copy in out_copies(i):
            copy.wait()


def shards(rows, cols, queries, keys, values, pattern):
    tokens, width = queries.shape
    half = width // cols
    chunks = half // (GROUP * HD)
    whole = tokens * cols
    dma = pltpu.SemaphoreType.DMA
    return pl.pallas_call(
        functools.partial(kernel, rows, cols),
        out_shape=jax.ShapeDtypeStruct((tokens, width), jnp.bfloat16),
        in_specs=[pl.BlockSpec(memory_space=pltpu.HBM)] * 3
        + [pl.BlockSpec(memory_space=pltpu.SMEM)],
        out_specs=pl.BlockSpec(memory_space=pltpu.VMEM),
        scratch_shapes=[
            pltpu.VMEM((whole, half), jnp.bfloat16),
            pltpu.VMEM((5, 2, whole, half), jnp.bfloat16),
            pltpu.VMEM((whole, half), jnp.bfloat16),
            pltpu.VMEM((GROUP, whole, HD), jnp.float32),
            pltpu.VMEM((GROUP, whole, 1), jnp.float32),
            pltpu.VMEM((GROUP, whole, 1), jnp.float32),
            dma((3, cols - 1, chunks)),
            dma((3, cols - 1, chunks)),
            dma((3, chunks)),
            dma((4, 2, cols, chunks)),
            dma((4, 2, cols, chunks)),
            dma((cols - 1, chunks)),
            dma((cols - 1, chunks)),
        ],
        compiler_params=pltpu.CompilerParams(
            collective_id=0, has_side_effects=True, vmem_limit_bytes=60 * 1024 * 1024
        ),
        cost_estimate=pl.CostEstimate(
            flops=4 * 4 * whole * whole * half,
            bytes_accessed=8 * tokens * width,
            transcendentals=4 * whole * whole * half // HD,
        ),
    )(queries, keys, values, pattern)


def solution(mesh):
    split = P(("groups", "row", "col"), None)
    return jax.shard_map(
        functools.partial(shards, mesh.shape["row"], mesh.shape["col"]),
        mesh=mesh,
        in_specs=(split, split, split, P("groups", None)),
        out_specs=split,
        check_vma=False,
    )
```

```python
import functools
import math

import jax
import jax.numpy as jnp
from jax import lax
from jax.experimental import pallas as pl
from jax.experimental.pallas import tpu as pltpu
from jax.sharding import PartitionSpec as P

HEADS = 20
HD = 128
TILE_H = 4
OFFSETS = (0, -1, 1, -TILE_H, TILE_H)
GROUP = 2

MESH = pl.DeviceIdType.MESH
FAR = 1e30
TO_EXP2 = math.log2(math.e) / math.sqrt(HD)


def kernel(
    rows, cols, q_hbm, k_hbm, v_hbm, pattern_hbm, out_ref,
    q_all, kv, staged, acc, top, total,
    pattern_ref, pattern_sem, near_send, near_recv, local_sem, far_send, far_recv, out_send, out_recv,
):
    row = lax.axis_index("row")
    col = lax.axis_index("col")
    tokens = q_hbm.shape[0]
    half = q_hbm.shape[1] // cols
    step = GROUP * HD
    chunks = half // step
    own_tokens = pl.ds(pl.multiple_of(col * tokens, tokens), tokens)

    def has(offset):
        if offset == -1:
            return lax.rem(row, TILE_H) != 0
        if offset == 1:
            return (lax.rem(row, TILE_H) != TILE_H - 1) & (row + 1 < rows)
        if offset < 0:
            return row >= -offset
        return row + offset < rows

    def other_col(d):
        return lax.rem(col + d, cols)

    def wide(which, i):
        return pl.ds(pl.multiple_of(which * half + i * step, HD), step)

    def narrow(i):
        return pl.ds(pl.multiple_of(i * step, HD), step)

    fetch = pltpu.make_async_copy(pattern_hbm, pattern_ref, pattern_sem)
    fetch.start()

    barrier = pltpu.get_barrier_semaphore()
    for d in range(1, cols):
        pl.semaphore_signal(barrier, inc=1, device_id={"col": other_col(d)}, device_id_type=MESH)
    for j in range(1, 5):
        @pl.when(has(-OFFSETS[j]))
        def _():
            for d in range(cols):
                pl.semaphore_signal(
                    barrier, inc=1,
                    device_id={"row": row - OFFSETS[j], "col": other_col(d)},
                    device_id_type=MESH,
                )
    peers = cols - 1
    for j in range(1, 5):
        peers = peers + cols * has(-OFFSETS[j]).astype(jnp.int32)
    pl.semaphore_wait(barrier, peers)

    def near_parts(i):
        return (
            (0, k_hbm, kv.at[0, 0, own_tokens, narrow(i)]),
            (1, v_hbm, kv.at[0, 1, own_tokens, narrow(i)]),
            (2, q_hbm, q_all.at[own_tokens, narrow(i)]),
        )

    def near_copies(i, which):
        for n, src, dst in near_parts(i):
            if n in which:
                for d in range(1, cols):
                    yield pltpu.make_async_remote_copy(
                        src_ref=src.at[:, wide(other_col(d), i)],
                        dst_ref=dst,
                        send_sem=near_send.at[n, d - 1, i],
                        recv_sem=near_recv.at[n, d - 1, i],
                        device_id={"col": other_col(d)},
                        device_id_type=MESH,
                    )

    def local_copies(i, which):
        for n, src, dst in near_parts(i):
            if n in which:
                yield pltpu.make_async_copy(
                    src.at[:, wide(col, i)], dst, local_sem.at[n, i]
                )

    def far_copies(j, i):
        for d in range(cols):
            for n, src in ((0, k_hbm), (1, v_hbm)):
                yield pltpu.make_async_remote_copy(
                    src_ref=src.at[:, wide(other_col(d), i)],
                    dst_ref=kv.at[j, n, own_tokens, narrow(i)],
                    send_sem=far_send.at[j - 1, n, d, i],
                    recv_sem=far_recv.at[j - 1, n, d, i],
                    device_id={"row": row - OFFSETS[j], "col": other_col(d)},
                    device_id_type=MESH,
                )

    @pl.loop(0, chunks)
    def _(i):
        for j in (3, 4):
            @pl.when(has(-OFFSETS[j]))
            def _():
                for copy in far_copies(j, i):
                    copy.start()

    @pl.loop(0, chunks)
    def _(i):
        for copy in near_copies(i, (0, 1, 2)):
            copy.start()
        for copy in local_copies(i, (0, 1, 2)):
            copy.start()

    @pl.loop(0, chunks)
    def _(i):
        for j in (1, 2):
            @pl.when(has(-OFFSETS[j]))
            def _():
                for copy in far_copies(j, i):
                    copy.start()

    fetch.wait()

    def out_copies(i):
        for d in range(1, cols):
            to = other_col(d)
            yield pltpu.make_async_remote_copy(
                src_ref=staged.at[pl.ds(pl.multiple_of(to * tokens, tokens), tokens), narrow(i)],
                dst_ref=out_ref.at[:, wide(col, i)],
                send_sem=out_send.at[d - 1, i],
                recv_sem=out_recv.at[d - 1, i],
                device_id={"col": to},
                device_id_type=MESH,
            )

    @pl.loop(0, chunks)
    def _(i):
        for copy in near_copies(i, (0, 1, 2)):
            copy.wait_recv()
        for copy in local_copies(i, (0, 1, 2)):
            copy.wait()

        def block(j, g):
            head = pl.ds(pl.multiple_of(i * step + g * HD, HD), HD)
            scores = lax.dot_general(
                q_all[:, head], kv[j, 0, :, head], (((1,), (1,)), ((), ())),
                preferred_element_type=jnp.float32,
            )
            peak = jnp.max(scores, axis=1, keepdims=True)
            if j == 0:
                weights = jnp.exp2((scores - peak) * TO_EXP2)
                here = jnp.sum(weights, axis=1, keepdims=True)
                out = jnp.dot(
                    weights.astype(jnp.bfloat16), kv[j, 1, :, head],
                    preferred_element_type=jnp.float32,
                )
                top[g] = peak
                total[g] = here
                acc[g] = out
            else:
                live = pattern_ref[row, j] == 1
                before = top[g]
                after = jnp.where(live, jnp.maximum(before, peak), before)
                weights = jnp.exp2((scores - jnp.where(live, after, FAR)) * TO_EXP2)
                here = jnp.sum(weights, axis=1, keepdims=True)
                out = jnp.dot(
                    weights.astype(jnp.bfloat16), kv[j, 1, :, head],
                    preferred_element_type=jnp.float32,
                )
                factor = jnp.exp2((before - after) * TO_EXP2)
                top[g] = after
                total[g] = total[g] * factor + here
                acc[g] = acc[g] * factor + out

        for g in range(GROUP):
            block(0, g)
        for j in (1, 2, 3, 4):
            @pl.when(has(OFFSETS[j]))
            def _():
                for copy in far_copies(j, i):
                    copy.wait_recv()
                for g in range(GROUP):
                    block(j, g)
        for g in range(GROUP):
            head = pl.ds(pl.multiple_of(i * step + g * HD, HD), HD)
            staged[:, head] = (acc[g] / total[g]).astype(jnp.bfloat16)
        out_ref[:, wide(col, i)] = staged[own_tokens, narrow(i)]
        for copy in out_copies(i):
            copy.start()

    @pl.loop(0, chunks)
    def _(i):
        for copy in near_copies(i, (0, 1, 2)):
            copy.wait_send()
        for j in range(1, 5):
            @pl.when(has(-OFFSETS[j]))
            def _():
                for copy in far_copies(j, i):
                    copy.wait_send()
        for copy in out_copies(i):
            copy.wait()


def shards(rows, cols, queries, keys, values, pattern):
    tokens, width = queries.shape
    half = width // cols
    chunks = half // (GROUP * HD)
    whole = tokens * cols
    dma = pltpu.SemaphoreType.DMA
    return pl.pallas_call(
        functools.partial(kernel, rows, cols),
        out_shape=jax.ShapeDtypeStruct((tokens, width), jnp.bfloat16),
        in_specs=[pl.BlockSpec(memory_space=pltpu.HBM)] * 3
        + [pl.BlockSpec(memory_space=pltpu.HBM)],
        out_specs=pl.BlockSpec(memory_space=pltpu.VMEM),
        scratch_shapes=[
            pltpu.VMEM((whole, half), jnp.bfloat16),
            pltpu.VMEM((5, 2, whole, half), jnp.bfloat16),
            pltpu.VMEM((whole, half), jnp.bfloat16),
            pltpu.VMEM((GROUP, whole, HD), jnp.float32),
            pltpu.VMEM((GROUP, whole, 1), jnp.float32),
            pltpu.VMEM((GROUP, whole, 1), jnp.float32),
            pltpu.SMEM(pattern.shape, pattern.dtype),
            dma(()),
            dma((3, cols - 1, chunks)),
            dma((3, cols - 1, chunks)),
            dma((3, chunks)),
            dma((4, 2, cols, chunks)),
            dma((4, 2, cols, chunks)),
            dma((cols - 1, chunks)),
            dma((cols - 1, chunks)),
        ],
        compiler_params=pltpu.CompilerParams(
            collective_id=0, has_side_effects=True, vmem_limit_bytes=60 * 1024 * 1024
        ),
        cost_estimate=pl.CostEstimate(
            flops=4 * 4 * whole * whole * half,
            bytes_accessed=8 * tokens * width,
            transcendentals=4 * whole * whole * half // HD,
        ),
    )(queries, keys, values, pattern)


def solution(mesh):
    split = P(("groups", "row", "col"), None)
    return jax.shard_map(
        functools.partial(shards, mesh.shape["row"], mesh.shape["col"]),
        mesh=mesh,
        in_specs=(split, split, split, P("groups", None)),
        out_specs=split,
        check_vma=False,
    )
```

```python
import functools
import math

import jax
import jax.numpy as jnp
from jax import lax
from jax.experimental import pallas as pl
from jax.experimental.pallas import tpu as pltpu
from jax.sharding import PartitionSpec as P

HEADS = 20
HD = 128
TILE_H = 4
OFFSETS = (0, -1, 1, -TILE_H, TILE_H)
GROUP = 2

MESH = pl.DeviceIdType.MESH
FAR = 1e30
TO_EXP2 = math.log2(math.e) / math.sqrt(HD)


def kernel(
    rows, cols, q_hbm, k_hbm, v_hbm, pattern_hbm, out_ref,
    q_all, kv, staged, acc, top, total,
    pattern_ref, pattern_sem, passed_send, near_send, near_recv, local_sem, far_send, far_recv, out_send, out_recv,
):
    row = lax.axis_index("row")
    col = lax.axis_index("col")
    tokens = q_hbm.shape[0]
    half = q_hbm.shape[1] // cols
    step = GROUP * HD
    chunks = half // step
    own_tokens = pl.ds(pl.multiple_of(col * tokens, tokens), tokens)

    def has(offset):
        if offset == -1:
            return lax.rem(row, TILE_H) != 0
        if offset == 1:
            return (lax.rem(row, TILE_H) != TILE_H - 1) & (row + 1 < rows)
        if offset < 0:
            return row >= -offset
        return row + offset < rows

    def other_col(d):
        return lax.rem(col + d, cols)

    def wide(which, i):
        return pl.ds(pl.multiple_of(which * half + i * step, HD), step)

    def narrow(i):
        return pl.ds(pl.multiple_of(i * step, HD), step)

    fetch = pltpu.make_async_copy(pattern_hbm, pattern_ref, pattern_sem)
    fetch.start()

    passed = chunks // 2 if TILE_H == 4 and rows % TILE_H == 0 else 0
    place = lax.rem(row, TILE_H)

    def sends(j, i):
        if j > 2 or passed == 0:
            return has(-OFFSETS[j])
        return has(-OFFSETS[j]) & ((place != j) | (i >= passed))

    def passes(j):
        return place == (TILE_H - 1 if j == 1 else 0)

    def pass_copies(j, i):
        for d in range(cols):
            for n in range(2):
                part = (n, pl.ds(d * tokens, tokens), narrow(i))
                yield pltpu.make_async_remote_copy(
                    src_ref=kv.at[(j,) + part],
                    dst_ref=kv.at[(3 - j,) + part],
                    send_sem=passed_send.at[n, d, i],
                    recv_sem=far_recv.at[2 - j, n, d, i],
                    device_id={"row": row + 2 * OFFSETS[j]},
                    device_id_type=MESH,
                )

    barrier = pltpu.get_barrier_semaphore()
    for d in range(1, cols):
        pl.semaphore_signal(barrier, inc=1, device_id={"col": other_col(d)}, device_id_type=MESH)
    for j in range(1, 5):
        @pl.when(has(-OFFSETS[j]))
        def _():
            for d in range(cols):
                pl.semaphore_signal(
                    barrier, inc=1,
                    device_id={"row": row - OFFSETS[j], "col": other_col(d)},
                    device_id_type=MESH,
                )
    peers = cols - 1
    if passed:
        for at, to in ((1, 2), (2, -2)):
            @pl.when(place == at)
            def _():
                pl.semaphore_signal(
                    barrier, inc=1, device_id={"row": row + to}, device_id_type=MESH
                )
        peers = peers + passes(1).astype(jnp.int32) + passes(2).astype(jnp.int32)
    for j in range(1, 5):
        peers = peers + cols * has(-OFFSETS[j]).astype(jnp.int32)
    pl.semaphore_wait(barrier, peers)

    def near_parts(i):
        return (
            (0, k_hbm, kv.at[0, 0, own_tokens, narrow(i)]),
            (1, v_hbm, kv.at[0, 1, own_tokens, narrow(i)]),
            (2, q_hbm, q_all.at[own_tokens, narrow(i)]),
        )

    def near_copies(i, which):
        for n, src, dst in near_parts(i):
            if n in which:
                for d in range(1, cols):
                    yield pltpu.make_async_remote_copy(
                        src_ref=src.at[:, wide(other_col(d), i)],
                        dst_ref=dst,
                        send_sem=near_send.at[n, d - 1, i],
                        recv_sem=near_recv.at[n, d - 1, i],
                        device_id={"col": other_col(d)},
                        device_id_type=MESH,
                    )

    def local_copies(i, which):
        for n, src, dst in near_parts(i):
            if n in which:
                yield pltpu.make_async_copy(
                    src.at[:, wide(col, i)], dst, local_sem.at[n, i]
                )

    def far_copies(j, i):
        for d in range(cols):
            for n, src in ((0, k_hbm), (1, v_hbm)):
                yield pltpu.make_async_remote_copy(
                    src_ref=src.at[:, wide(other_col(d), i)],
                    dst_ref=kv.at[j, n, own_tokens, narrow(i)],
                    send_sem=far_send.at[j - 1, n, d, i],
                    recv_sem=far_recv.at[j - 1, n, d, i],
                    device_id={"row": row - OFFSETS[j], "col": other_col(d)},
                    device_id_type=MESH,
                )

    @pl.loop(0, chunks)
    def _(i):
        for j in (3, 4):
            @pl.when(has(-OFFSETS[j]))
            def _():
                for copy in far_copies(j, i):
                    copy.start()

    @pl.loop(0, chunks)
    def _(i):
        for copy in near_copies(i, (0, 1, 2)):
            copy.start()
        for copy in local_copies(i, (0, 1, 2)):
            copy.start()

    @pl.loop(0, chunks)
    def _(i):
        for j in (1, 2):
            @pl.when(sends(j, i))
            def _():
                for copy in far_copies(j, i):
                    copy.start()

    fetch.wait()

    def out_copies(i):
        for d in range(1, cols):
            to = other_col(d)
            yield pltpu.make_async_remote_copy(
                src_ref=staged.at[pl.ds(pl.multiple_of(to * tokens, tokens), tokens), narrow(i)],
                dst_ref=out_ref.at[:, wide(col, i)],
                send_sem=out_send.at[d - 1, i],
                recv_sem=out_recv.at[d - 1, i],
                device_id={"col": to},
                device_id_type=MESH,
            )

    @pl.loop(0, chunks)
    def _(i):
        for copy in near_copies(i, (0, 1, 2)):
            copy.wait_recv()
        for copy in local_copies(i, (0, 1, 2)):
            copy.wait()

        def block(j, g):
            head = pl.ds(pl.multiple_of(i * step + g * HD, HD), HD)
            scores = lax.dot_general(
                q_all[:, head], kv[j, 0, :, head], (((1,), (1,)), ((), ())),
                preferred_element_type=jnp.float32,
            )
            peak = jnp.max(scores, axis=1, keepdims=True)
            if j == 0:
                weights = jnp.exp2((scores - peak) * TO_EXP2)
                here = jnp.sum(weights, axis=1, keepdims=True)
                out = jnp.dot(
                    weights.astype(jnp.bfloat16), kv[j, 1, :, head],
                    preferred_element_type=jnp.float32,
                )
                top[g] = peak
                total[g] = here
                acc[g] = out
            else:
                live = pattern_ref[row, j] == 1
                before = top[g]
                after = jnp.where(live, jnp.maximum(before, peak), before)
                weights = jnp.exp2((scores - jnp.where(live, after, FAR)) * TO_EXP2)
                here = jnp.sum(weights, axis=1, keepdims=True)
                out = jnp.dot(
                    weights.astype(jnp.bfloat16), kv[j, 1, :, head],
                    preferred_element_type=jnp.float32,
                )
                factor = jnp.exp2((before - after) * TO_EXP2)
                top[g] = after
                total[g] = total[g] * factor + here
                acc[g] = acc[g] * factor + out

        for g in range(GROUP):
            block(0, g)
        for j in (1, 2, 3, 4):
            @pl.when(has(OFFSETS[j]))
            def _():
                for copy in far_copies(j, i):
                    copy.wait_recv()
                if j in (1, 2):
                    @pl.when(passes(j) & (i < passed))
                    def _():
                        for copy in pass_copies(j, i):
                            copy.start()
                for g in range(GROUP):
                    block(j, g)
        for g in range(GROUP):
            head = pl.ds(pl.multiple_of(i * step + g * HD, HD), HD)
            staged[:, head] = (acc[g] / total[g]).astype(jnp.bfloat16)
        out_ref[:, wide(col, i)] = staged[own_tokens, narrow(i)]
        for copy in out_copies(i):
            copy.start()

    @pl.loop(0, chunks)
    def _(i):
        for copy in near_copies(i, (0, 1, 2)):
            copy.wait_send()
        for j in range(1, 5):
            @pl.when(sends(j, i))
            def _():
                for copy in far_copies(j, i):
                    copy.wait_send()
        for j in (1, 2):
            @pl.when(passes(j) & (i < passed))
            def _():
                for copy in pass_copies(j, i):
                    copy.wait_send()
        for copy in out_copies(i):
            copy.wait()


def shards(rows, cols, queries, keys, values, pattern):
    tokens, width = queries.shape
    half = width // cols
    chunks = half // (GROUP * HD)
    whole = tokens * cols
    dma = pltpu.SemaphoreType.DMA
    return pl.pallas_call(
        functools.partial(kernel, rows, cols),
        out_shape=jax.ShapeDtypeStruct((tokens, width), jnp.bfloat16),
        in_specs=[pl.BlockSpec(memory_space=pltpu.HBM)] * 3
        + [pl.BlockSpec(memory_space=pltpu.HBM)],
        out_specs=pl.BlockSpec(memory_space=pltpu.VMEM),
        scratch_shapes=[
            pltpu.VMEM((whole, half), jnp.bfloat16),
            pltpu.VMEM((5, 2, whole, half), jnp.bfloat16),
            pltpu.VMEM((whole, half), jnp.bfloat16),
            pltpu.VMEM((GROUP, whole, HD), jnp.float32),
            pltpu.VMEM((GROUP, whole, 1), jnp.float32),
            pltpu.VMEM((GROUP, whole, 1), jnp.float32),
            pltpu.SMEM(pattern.shape, pattern.dtype),
            dma(()),
            dma((2, cols, chunks)),
            dma((3, cols - 1, chunks)),
            dma((3, cols - 1, chunks)),
            dma((3, chunks)),
            dma((4, 2, cols, chunks)),
            dma((4, 2, cols, chunks)),
            dma((cols - 1, chunks)),
            dma((cols - 1, chunks)),
        ],
        compiler_params=pltpu.CompilerParams(
            collective_id=0, has_side_effects=True, vmem_limit_bytes=60 * 1024 * 1024
        ),
        cost_estimate=pl.CostEstimate(
            flops=4 * 4 * whole * whole * half,
            bytes_accessed=8 * tokens * width,
            transcendentals=4 * whole * whole * half // HD,
        ),
    )(queries, keys, values, pattern)


def solution(mesh):
    split = P(("groups", "row", "col"), None)
    return jax.shard_map(
        functools.partial(shards, mesh.shape["row"], mesh.shape["col"]),
        mesh=mesh,
        in_specs=(split, split, split, P("groups", None)),
        out_specs=split,
        check_vma=False,
    )
```
